768 devices in a mesh: seq: 48 (over x, z_lo, core), mp: 16 (over z_hi, y).
Axes of the slice: x: 4, y: 8, z: 12 (z_hi: 2, z_lo: 6; z = z_hi * 6 + z_lo), core: 2. Of those that a mesh axis runs over, the one named last changes fastest.
Arguments:
- vit_hidden: bfloat16 [12288, 3200], P('seq'), may hold values from -6 to 6
- vit_gain: float32 [3200], replicated, may hold values from 0.5 to 1.5
- vit_bias: float32 [3200], replicated, may hold values from -3 to 3
- proj_weight: bfloat16 [3200, 8192], P(None, 'mp'), may hold values from -0.109375 to 0.109375
- text_emb: bfloat16 [24576, 8192], P('seq', 'mp'), may hold values from -40 to 40
- llm_gain: float32 [8192], P('mp'), may hold values from 0.5 to 1.5
- cotangent: bfloat16 [24576, 8192], P('seq', 'mp'), may hold values from -6 to 6
- tile_start: int32 [48], replicated, may hold values from 0 to 3040, as said below
- tile_owner: int32 [48], replicated, may hold values from 0 to 47, each once
Outputs:
- normed: bfloat16 [24576, 8192], P('seq', 'mp')
- grad_text: bfloat16 [24576, 8192], P('seq', 'mp')
- grad_vit: bfloat16 [12288, 3200], P('seq', 'mp')
The draws below stay inside these ranges and needn't reach their ends.
Inputs may be any that keep to these rules, and one draw needn't show every extreme that they name: `tile_start`: starts increase with the tile's index and tiles never intersect; tile 0 begins the packed stretch and the last tile ends it.
All inputs are finite; a program needn't handle non-finite values.
Results may differ from the reference program's by a relative error of at most 0.0015.
The reference program's roundings to bfloat16 on the way (of `normed_vit`, `image_embed`, `merged` and `grad_embed`) count: a program that leaves them out, or rounds other values in their place, can miss the bound.
Values may be sent and summed in bfloat16 or wider, within the bound.
A program may use at most 32 MiB of HBM per device.

```python
import jax
import jax.numpy as jnp
from jax import lax

D = 8192
DV = 3200
BLK = 8
TILE_BLOCKS = 32
LOCAL_BLOCKS = 64
TILES = 48
VROWS = 12288
TOKENS = 24576
SEQ_BLOCKS = 3072
TEXT_BLOCKS = 1536


def draw_text_emb(key, part):
    base_key = jax.random.fold_in(key, 11)
    first_key, second_key, third_key = jax.random.split(base_key, 3)
    columns = jnp.arange(D, dtype=jnp.float32) / D
    column_scale = 0.3 * jnp.exp(columns * jnp.log(3.0)) * jnp.exp(jax.random.uniform(second_key, (D,), jnp.float32, 0.0, jnp.log(3.0)))
    row_scale = jnp.exp(jax.random.uniform(third_key, (TOKENS, 1), jnp.float32, jnp.log(0.35), jnp.log(3.5)))
    base = jnp.clip(jax.random.normal(first_key, (TOKENS, D), jnp.float32), -4.0, 4.0)
    return (base * column_scale * row_scale).astype(jnp.bfloat16)


def draw_tile_start(key, part):
    gap_key = jax.random.fold_in(key, 23)
    gaps = jax.random.randint(gap_key, (TILES,), 0, TEXT_BLOCKS + 1)
    gaps = jnp.sort(gaps)
    gaps = gaps.at[0].set(0).at[TILES - 1].set(TEXT_BLOCKS)
    return (gaps + TILE_BLOCKS * jnp.arange(TILES)).astype(jnp.int32)


def shard_levels(rng, extent, cuts, smallest, high):
    def one(dim, shards_of):
        heights = jax.random.uniform(jax.random.fold_in(jax.random.fold_in(rng, 6), dim), (shards_of,), jnp.float32, smallest / len(cuts), high / len(cuts))
        return jnp.repeat(jnp.exp(heights), extent[dim] // shards_of).reshape((-1,) + (1,) * (len(extent) - dim - 1))

    level = one(*cuts[0])
    for cut in cuts[1:]:
        level = level * one(*cut)
    return level


def bell_draw(own_key, extent, scale, most, cuts=(), kind=jnp.bfloat16):
    array = scale * jax.random.normal(own_key, extent, jnp.float32)
    if cuts:
        array = array * shard_levels(own_key, extent, cuts, -0.22, 0.18)
    return jnp.clip(array, -most, most).astype(kind)


def setup_inputs(seed: int = 0) -> dict:
    arg_keys = jax.random.split(jax.random.key(seed), 10)
    vit_hidden = bell_draw(arg_keys[0], (VROWS, DV), 1.0, 6.0, ((0, 48),))
    vit_gain = jnp.clip(1.0 + 0.1 * jax.random.normal(arg_keys[1], (DV,), jnp.float32), 0.5, 1.5)
    vit_bias = bell_draw(arg_keys[2], (DV,), 0.5, 3.0, (), jnp.float32)
    proj_weight = bell_draw(arg_keys[3], (DV, D), DV ** -0.5, 0.109375, ((1, 16),))
    text_emb = draw_text_emb(jax.random.fold_in(arg_keys[9], 71), 0)
    llm_gain = jnp.clip(1.0 + 0.1 * jax.random.normal(arg_keys[5], (D,), jnp.float32), 0.5, 1.5)
    cotangent = bell_draw(arg_keys[6], (TOKENS, D), 1.0, 6.0, ((0, 48), (1, 16)))
    tile_start = draw_tile_start(jax.random.fold_in(arg_keys[9], 71), 0)
    tile_owner = jax.random.permutation(arg_keys[8], TILES).astype(jnp.int32)
    return {"vit_hidden": vit_hidden, "vit_gain": vit_gain, "vit_bias": vit_bias, "proj_weight": proj_weight, "text_emb": text_emb, "llm_gain": llm_gain, "cotangent": cotangent, "tile_start": tile_start, "tile_owner": tile_owner}


EPSILON = 1e-05

def reference(vit_hidden, vit_gain, vit_bias, proj_weight, text_emb, llm_gain, cotangent, tile_start, tile_owner):
    values = vit_hidden.astype(jnp.float32)
    centred = values - lax.optimization_barrier(jnp.mean(values, axis=1, keepdims=True))
    inv_std = lax.rsqrt(lax.optimization_barrier(jnp.mean(centred * centred, axis=1, keepdims=True)) + EPSILON)
    unit_rows = centred * inv_std
    normed_vit = (unit_rows * vit_gain + vit_bias).astype(jnp.bfloat16)
    image_embed = jnp.dot(normed_vit, proj_weight, preferred_element_type=jnp.float32).astype(jnp.bfloat16)
    row_block = jnp.arange(SEQ_BLOCKS, dtype=jnp.int32)
    global_block = (row_block % LOCAL_BLOCKS * TILES + row_block // LOCAL_BLOCKS).astype(jnp.int32)
    started = (tile_start[None, :] <= global_block[:, None]).astype(jnp.int32)
    found = (lax.optimization_barrier(jnp.sum(started, axis=1)) - 1).astype(jnp.int32)
    tile_index = jnp.maximum(found, 0).astype(jnp.int32)
    offset = (global_block - jnp.take(tile_start, tile_index)).astype(jnp.int32)
    inside = (found >= 0) & (offset < TILE_BLOCKS)
    source = jnp.where(inside, jnp.take(tile_owner, tile_index) * TILE_BLOCKS + offset, 0).astype(jnp.int32)
    embed_blocks = image_embed.reshape(TILES * TILE_BLOCKS, BLK, D)
    text_blocks = text_emb.reshape(SEQ_BLOCKS, BLK, D)
    merged = jnp.where(inside[:, None, None], jnp.take(embed_blocks, source, axis=0), text_blocks).reshape(TOKENS, D)
    merged_f = merged.astype(jnp.float32)
    grad_gain = llm_gain * cotangent.astype(jnp.float32)
    squares = lax.optimization_barrier(jnp.sum(merged_f * merged_f, axis=1))
    products = lax.optimization_barrier(jnp.sum(grad_gain * merged_f, axis=1))
    inv_rms = lax.rsqrt(squares / D + EPSILON)
    normed = (merged_f * inv_rms[:, None] * llm_gain).astype(jnp.bfloat16)
    grad_merged = inv_rms[:, None] * grad_gain - merged_f * (inv_rms * inv_rms * inv_rms * products / D)[:, None]
    image_rows = jnp.repeat(inside, BLK)
    grad_text = jnp.where(image_rows[:, None], 0.0, grad_merged).astype(jnp.bfloat16)
    grad_blocks = grad_merged.astype(jnp.bfloat16).reshape(SEQ_BLOCKS, BLK, D)
    target = jnp.where(inside, source, TILES * TILE_BLOCKS).astype(jnp.int32)
    grad_embed = jnp.zeros((TILES * TILE_BLOCKS, BLK, D), jnp.bfloat16).at[target].set(grad_blocks, mode='drop').reshape(VROWS, D)
    grad_normed = jnp.dot(grad_embed, proj_weight.T, preferred_element_type=jnp.float32)
    scaled = grad_normed * vit_gain
    first = lax.optimization_barrier(jnp.mean(scaled, axis=1, keepdims=True))
    second = lax.optimization_barrier(jnp.mean(scaled * unit_rows, axis=1, keepdims=True))
    grad_vit = (inv_std * (scaled - first - unit_rows * second)).astype(jnp.bfloat16)
    return (normed, grad_text, grad_vit)
```

```python
import functools

import jax
import jax.numpy as jnp
from jax import lax
from jax.experimental import pallas as pl
from jax.experimental.pallas import tpu as pltpu
from jax.sharding import PartitionSpec as P

BLK = 8
EPSILON = 1e-05
F32 = jnp.float32
BF16 = jnp.bfloat16
MESH = pl.DeviceIdType.MESH
NT = (((1,), (1,)), ((), ()))


def three_parts(x):
    hi = x.astype(BF16).astype(F32)
    mid = (x - hi).astype(BF16).astype(F32)
    return hi, mid, (x - hi) - mid


def stacked(parts, rows, width):
    row = lax.broadcasted_iota(jnp.int32, (rows, width), 0)
    out = jnp.zeros((rows, width), F32)
    for i, part in enumerate(parts):
        out = jnp.where(row == i, jnp.broadcast_to(part, (rows, width)), out)
    return out.astype(BF16)


def folded(x):
    half = x.shape[1] // 2
    return jnp.concatenate([x[:, :half], x[:, half:]], axis=0)


def unfolded(x):
    return jnp.concatenate([x[:BLK], x[BLK:]], axis=1)


def coded(x):
    most = jnp.max(jnp.abs(x), axis=0, keepdims=True)
    exponent = jnp.ceil(jnp.log2(jnp.maximum(most, 1e-30) * 1.0001)) - 15.0
    codes = jnp.clip(jnp.round(x * jnp.exp2(-exponent)), -32767.0, 32767.0)
    below = jnp.broadcast_to(exponent, (8, x.shape[1]))
    return jnp.concatenate([codes, below], axis=0).astype(jnp.int32).astype(jnp.int16)


def decoded(q):
    values = q.astype(jnp.int32).astype(F32)
    rows = q.shape[0] - 8
    return values[:rows] * jnp.exp2(values[rows : rows + 1])


def kernel(
    seq, ny, full_width,
    maps, vit_hbm, gain_ref, bias_ref, weight_hbm, text_hbm, llm_ref, cot_hbm,
    normed_hbm, gtext_hbm, gvit_hbm,
    vit, weight, text, cot, normed_v, gtext_v, gvit_v,
    nvit, colstat, rowstat, pre, select, hid_t, gain_col,
    out_buf, in_buf, merged, grads, back_out, back_in, gembed, partial,
    stat_out, stat_in, mean_out, mean_in, ring_out, ring_in, z_out, z_in,
    local_sem, store_sem, a2a_send, a2a_recv, back_send, back_recv,
    stat_send, stat_recv, mean_send, mean_recv, ring_send, ring_recv, z_send, z_recv,
):
    mp = 2 * ny
    me = lax.axis_index("seq")
    rank = lax.axis_index("mp")
    zh = rank // ny
    y = rank % ny
    rows, features = vit.shape
    width = weight.shape[1]
    tile_blocks = rows // BLK
    local_blocks = text.shape[0] // BLK
    share = features // mp
    half = ny // 2

    barrier = pltpu.get_barrier_semaphore()

    loads = [
        pltpu.make_async_copy(vit_hbm, vit, local_sem.at[0]),
        pltpu.make_async_copy(weight_hbm, weight, local_sem.at[1]),
        pltpu.make_async_copy(text_hbm, text, local_sem.at[2]),
        pltpu.make_async_copy(cot_hbm, cot, local_sem.at[3]),
    ]
    for load in loads:
        load.start()

    def greet_seq(i, carry):
        pl.semaphore_signal(barrier, inc=1, device_id={"seq": lax.rem(me + i, seq)}, device_id_type=MESH)
        return carry

    def greet_mp(i, carry):
        pl.semaphore_signal(barrier, inc=1, device_id={"mp": lax.rem(rank + i, mp)}, device_id_type=MESH)
        return carry

    lax.fori_loop(1, seq, greet_seq, 0)
    lax.fori_loop(1, mp, greet_mp, 0)

    loads[0].wait()
    gain = gain_ref[...]
    bias = bias_ref[...]
    lane16 = lax.broadcasted_iota(jnp.int32, (16, 128), 1)

    def norm_rows(i, carry):
        at = pl.ds(pl.multiple_of(i * 16, 16), 16)
        x = vit[at, :].astype(F32)
        mean = jnp.sum(x, axis=1, keepdims=True) / features
        centred = x - mean
        inv = lax.rsqrt(jnp.sum(centred * centred, axis=1, keepdims=True) / features + EPSILON)
        nvit[at, :] = (centred * inv * gain + bias).astype(BF16)
        colstat[at, :] = jnp.where(lane16 == 0, mean, inv)
        return carry

    lax.fori_loop(0, rows // 16, norm_rows, 0)
    nvit[rows : rows + 16, :] = stacked(three_parts(gain) + three_parts(bias), 16, features)

    loads[1].wait()
    for n in range(2):
        cols = slice(n * (width // 2), (n + 1) * (width // 2))
        product = jnp.dot(nvit[...], weight[:, cols], preferred_element_type=F32)
        pre[:, :, cols] = product.reshape(tile_blocks + 2, BLK, width // 2)

    pl.semaphore_wait(barrier, seq - 1 + mp - 1)

    own_start = maps[local_blocks + me]

    def block_for(target):
        block = lax.rem(target - lax.rem(own_start, seq) + seq, seq)
        return folded(pre[jnp.minimum(block, tile_blocks - 1)]).astype(BF16)

    def send_block(i, carry):
        target = lax.rem(me + i, seq)
        out_buf[target] = block_for(target)
        pltpu.make_async_remote_copy(
            src_ref=out_buf.at[target], dst_ref=in_buf.at[me], send_sem=a2a_send, recv_sem=a2a_recv,
            device_id={"seq": target}, device_id_type=MESH,
        ).start()
        return carry

    lax.fori_loop(1, seq, send_block, 0)
    in_buf[me] = block_for(me)

    column = lax.broadcasted_iota(jnp.int32, (BLK, features), 1)
    within = lax.broadcasted_iota(jnp.int32, (BLK, features), 0)
    select_rows = select.shape[0]

    def pick_rows(i, carry):
        halves = []
        for h in range(2):
            hit = column == rank * share + i * 16 + h * 8 + within
            halves.append(jnp.where(hit, 1.0, 0.0))
            value = jnp.sum(jnp.where(hit, jnp.broadcast_to(gain, hit.shape), 0.0), axis=1, keepdims=True)
            gain_col[pl.ds(pl.multiple_of(i * 16 + h * 8, 8), 8), :] = jnp.broadcast_to(value, (BLK, 128))
        select[pl.ds(pl.multiple_of(i * 16, 16), 16), :] = jnp.concatenate(halves, axis=0).astype(BF16)
        return carry

    lax.fori_loop(0, select_rows // 16, pick_rows, 0)
    hid_t[...] = lax.dot_general(select[...], vit[...], NT, preferred_element_type=F32)
    rowstat[...] = jnp.transpose(colstat[...])[:8]

    loads[2].wait()
    loads[3].wait()
    waiting = in_buf.at[pl.ds(0, seq - 1)]
    pltpu.make_async_copy(waiting, waiting, a2a_recv).wait()

    llm = llm_ref[...]
    lane = lax.broadcasted_iota(jnp.int32, (BLK, 128), 1)

    def merge_pair(i, sums):
        at = pl.ds(pl.multiple_of(i * 16, 16), 16)
        text_pair = text[at, :].astype(F32)
        cot_pair = cot[at, :].astype(F32)
        for h in range(2):
            b = i * 2 + h
            source = maps[b]
            arrived = unfolded(in_buf[jnp.maximum(source, 0)].astype(F32))
            is_image = jnp.full((BLK, width), source, jnp.int32) >= 0
            m = jnp.where(is_image, arrived, text_pair[h * 8 : h * 8 + 8])
            merged[b] = m
            square = jnp.sum(m * m, axis=1, keepdims=True)
            product = jnp.sum(llm * cot_pair[h * 8 : h * 8 + 8] * m, axis=1, keepdims=True)
            sums = jnp.where(lane == b, square, sums)
            sums = jnp.where(lane == b + 64, product, sums)
        return sums

    stat_out[...] = lax.fori_loop(0, local_blocks // 2, merge_pair, jnp.ones((BLK, 128), F32))

    def send_stat(i, carry):
        target = lax.rem(rank + i, mp)
        pltpu.make_async_remote_copy(
            src_ref=stat_out, dst_ref=stat_in.at[rank], send_sem=stat_send, recv_sem=stat_recv,
            device_id={"mp": target}, device_id_type=MESH,
        ).start()
        return carry

    lax.fori_loop(1, mp, send_stat, 0)
    stat_in[rank] = stat_out[...]
    waiting = stat_in.at[pl.ds(0, mp - 1)]
    pltpu.make_async_copy(waiting, waiting, stat_recv).wait()

    total = stat_in[0]
    for i in range(1, mp):
        total = total + stat_in[i]
    inv_all = lax.rsqrt(total / full_width + EPSILON)
    slope_all = inv_all * inv_all * inv_all * pltpu.roll(total, 64, 1) / full_width

    def norm_pair(i, carry):
        at = pl.ds(pl.multiple_of(i * 16, 16), 16)
        cot_pair = cot[at, :].astype(F32)
        normed_pair, text_pair = [], []
        for h in range(2):
            b = i * 2 + h
            inv = jnp.sum(jnp.where(lane == b, inv_all, 0.0), axis=1, keepdims=True)
            slope = jnp.sum(jnp.where(lane == b, slope_all, 0.0), axis=1, keepdims=True)
            m = merged[b]
            normed_pair.append(m * inv * llm)
            grad = inv * (llm * cot_pair[h * 8 : h * 8 + 8]) - m * slope
            grads[b] = folded(grad).astype(BF16)
            is_image = jnp.full((BLK, width), maps[b], jnp.int32) >= 0
            text_pair.append(jnp.where(is_image, 0.0, grad))
        normed_v[at, :] = jnp.concatenate(normed_pair, axis=0).astype(BF16)
        gtext_v[at, :] = jnp.concatenate(text_pair, axis=0).astype(BF16)
        return carry

    lax.fori_loop(0, local_blocks // 2, norm_pair, 0)

    def grad_for(target):
        start = maps[local_blocks + target]
        block = start + lax.rem(me - lax.rem(start, seq) + seq, seq)
        return grads[jnp.minimum(block // seq, local_blocks - 1)]

    def send_back(i, carry):
        target = lax.rem(me + i, seq)
        back_out[target] = grad_for(target)
        pltpu.make_async_remote_copy(
            src_ref=back_out.at[target], dst_ref=back_in.at[me], send_sem=back_send, recv_sem=back_recv,
            device_id={"seq": target}, device_id_type=MESH,
        ).start()
        return carry

    lax.fori_loop(1, seq, send_back, 0)
    back_in[me] = grad_for(me)

    stores = [
        pltpu.make_async_copy(normed_v, normed_hbm, store_sem.at[0]),
        pltpu.make_async_copy(gtext_v, gtext_hbm, store_sem.at[1]),
    ]
    for store in stores:
        store.start()

    waiting = back_in.at[pl.ds(0, seq - 1)]
    pltpu.make_async_copy(waiting, waiting, back_recv).wait()

    def gather_pair(i, carry):
        pair = []
        for h in range(2):
            source = lax.rem(lax.rem(own_start, seq) + i * 2 + h, seq)
            pair.append(unfolded(back_in[source].astype(F32)))
        gembed[pl.ds(pl.multiple_of(i * 16, 16), 16), :] = jnp.concatenate(pair, axis=0).astype(BF16)
        return carry

    lax.fori_loop(0, tile_blocks // 2, gather_pair, 0)

    below = pre[tile_blocks]
    gain_weight = below[0:1] + below[1:2] + below[2:3]
    bias_weight = below[3:4] + below[4:5] + below[5:6]
    g = gembed[...]
    first = lax.dot_general(stacked(three_parts(gain_weight), 16, width), g, NT, preferred_element_type=F32)
    embed = pre[:tile_blocks].reshape(rows, width) - bias_weight
    weighted = g.astype(F32) * embed
    high = weighted.astype(BF16)
    low = (weighted - high.astype(F32)).astype(BF16)
    ones = jnp.ones((16, width), BF16)
    second = lax.dot_general(ones, high, NT, preferred_element_type=F32)
    second = second + lax.dot_general(ones, low, NT, preferred_element_type=F32)
    mean_out[...] = jnp.concatenate(
        [jnp.broadcast_to(jnp.sum(first, axis=0, keepdims=True), (8, rows)), second[:8]], axis=1
    )

    def send_mean(i, carry):
        target = lax.rem(rank + i, mp)
        pltpu.make_async_remote_copy(
            src_ref=mean_out, dst_ref=mean_in.at[rank], send_sem=mean_send, recv_sem=mean_recv,
            device_id={"mp": target}, device_id_type=MESH,
        ).start()
        return carry

    lax.fori_loop(1, mp, send_mean, 0)
    mean_in[rank] = mean_out[...]

    step_rows = features // 8
    for n in range(8):
        piece = slice(n * step_rows, (n + 1) * step_rows)
        partial[piece, :] = lax.dot_general(weight[piece, :], g, NT, preferred_element_type=F32)

    def own(target, h):
        start = (h * ny + target) * share
        return partial[pl.ds(pl.multiple_of(start, 8), share), :]

    def ring_copy(direction, step, h):
        to = lax.rem(y + 1, ny) if direction == 0 else lax.rem(y + ny - 1, ny)
        return pltpu.make_async_remote_copy(
            src_ref=ring_out.at[direction, step, h], dst_ref=ring_in.at[direction, step, h],
            send_sem=ring_send.at[direction, step, h], recv_sem=ring_recv.at[direction, step, h],
            device_id={"mp": zh * ny + to}, device_id_type=MESH,
        )

    copies = []
    for step in range(half):
        for h in range(2):
            for direction in range(2):
                if step == 0 and h != direction:
                    continue
                away = half - step
                target = lax.rem(y + away, ny) if direction == 0 else lax.rem(y + ny - away, ny)
                value = own(target, h)
                if step >= 2 or (step == 1 and h == direction):
                    ring_copy(direction, step - 1, h).wait_recv()
                    value = value + decoded(ring_in[direction, step - 1, h])
                ring_out[direction, step, h] = coded(value)
                copy = ring_copy(direction, step, h)
                copy.start()
                copies.append(copy)

    def arrived_sum(h):
        value = own(y, h)
        for direction in range(2):
            if half >= 2 or h == direction:
                ring_copy(direction, half - 1, h).wait_recv()
                value = value + decoded(ring_in[direction, half - 1, h])
        return value

    sums = [arrived_sum(h) for h in range(2)]
    z_out[...] = coded(jnp.where(jnp.full(sums[0].shape, zh, jnp.int32) == 0, sums[1], sums[0]))
    z_copy = pltpu.make_async_remote_copy(
        src_ref=z_out, dst_ref=z_in, send_sem=z_send, recv_sem=z_recv,
        device_id={"mp": (1 - zh) * ny + y}, device_id_type=MESH,
    )
    z_copy.start()
    kept = jnp.where(jnp.full(sums[0].shape, zh, jnp.int32) == 0, sums[0], sums[1])

    waiting = mean_in.at[pl.ds(0, mp - 1)]
    pltpu.make_async_copy(waiting, waiting, mean_recv).wait()
    means = mean_in[0]
    for i in range(1, mp):
        means = means + mean_in[i]
    means = means / features
    mean_first = means[0:1, :rows]
    mean_second = means[0:1, rows:]
    inv_row = rowstat[1:2, :]
    unit = (hid_t[:share, :] - rowstat[0:1, :]) * inv_row
    offset = mean_first + unit * mean_second
    z_copy.wait_recv()
    scaled = (kept + decoded(z_in[...])) * gain_col[:share, 0:1]
    result = inv_row * (scaled - offset)
    padded = jnp.concatenate([result, jnp.zeros((gvit_v.shape[1] - share, rows), F32)], axis=0)
    gvit_v[...] = jnp.transpose(padded).astype(BF16)
    last = pltpu.make_async_copy(gvit_v, gvit_hbm, store_sem.at[2])
    last.start()

    waiting = out_buf.at[pl.ds(0, seq - 1)]
    pltpu.make_async_copy(waiting, waiting, a2a_send).wait()
    waiting = back_out.at[pl.ds(0, seq - 1)]
    pltpu.make_async_copy(waiting, waiting, back_send).wait()
    waiting = stat_in.at[pl.ds(0, mp - 1)]
    pltpu.make_async_copy(waiting, waiting, stat_send).wait()
    waiting = mean_in.at[pl.ds(0, mp - 1)]
    pltpu.make_async_copy(waiting, waiting, mean_send).wait()
    for copy in copies:
        copy.wait_send()
    z_copy.wait_send()
    for store in stores:
        store.wait()
    last.wait()


def body(
    vit_hidden,
    vit_gain,
    vit_bias,
    proj_weight,
    text_emb,
    llm_gain,
    cotangent,
    tile_start,
    tile_owner,
):
    seq = lax.axis_size("seq")
    mp = lax.axis_size("mp")
    ny = mp // 2
    me = lax.axis_index("seq")
    rows, features = vit_hidden.shape
    width = proj_weight.shape[1]
    tokens = text_emb.shape[0]
    tile_blocks = rows // BLK
    local_blocks = tokens // BLK
    share = features // mp
    padded = -(-share // 128) * 128

    entry = jnp.arange(local_blocks + seq, dtype=jnp.int32)[:, None]
    start = tile_start[None, :]
    owner = tile_owner[None, :]
    away = (me - start) % seq
    slot = (start + away) // seq
    here = (away < tile_blocks) & (slot == entry)
    maps = jnp.sum(
        jnp.where(
            entry < local_blocks,
            jnp.where(here, owner + 1, 0),
            jnp.where(owner == entry - local_blocks, start, 0),
        ),
        axis=1,
    ) - jnp.where(entry[:, 0] < local_blocks, 1, 0)
    maps = maps.astype(jnp.int32)

    vmem = pl.BlockSpec(memory_space=pltpu.VMEM)
    anywhere = pl.BlockSpec(memory_space=pl.ANY)
    half_width = width // 2
    half = ny // 2
    dma = pltpu.SemaphoreType.DMA
    normed, grad_text, grad_vit = pl.pallas_call(
        functools.partial(kernel, seq, ny, width * mp),
        out_shape=(
            jax.ShapeDtypeStruct((tokens, width), BF16),
            jax.ShapeDtypeStruct((tokens, width), BF16),
            jax.ShapeDtypeStruct((rows, padded), BF16),
        ),
        in_specs=[
            pl.BlockSpec(memory_space=pltpu.SMEM),
            anywhere, vmem, vmem, anywhere, anywhere, vmem, anywhere,
        ],
        out_specs=(anywhere, anywhere, anywhere),
        scratch_shapes=[
            pltpu.VMEM((rows, features), BF16),
            pltpu.VMEM((features, width), BF16),
            pltpu.VMEM((tokens, width), BF16),
            pltpu.VMEM((tokens, width), BF16),
            pltpu.VMEM((tokens, width), BF16),
            pltpu.VMEM((tokens, width), BF16),
            pltpu.VMEM((rows, padded), BF16),
            pltpu.VMEM((rows + 16, features), BF16),
            pltpu.VMEM((rows, 128), F32),
            pltpu.VMEM((8, rows), F32),
            pltpu.VMEM((tile_blocks + 2, BLK, width), F32),
            pltpu.VMEM((-(-share // 16) * 16, features), BF16),
            pltpu.VMEM((-(-share // 16) * 16, rows), F32),
            pltpu.VMEM((-(-share // 16) * 16, 128), F32),
            pltpu.VMEM((seq, 16, half_width), BF16),
            pltpu.VMEM((seq, 16, half_width), BF16),
            pltpu.VMEM((local_blocks, BLK, width), F32),
            pltpu.VMEM((local_blocks, 16, half_width), BF16),
            pltpu.VMEM((seq, 16, half_width), BF16),
            pltpu.VMEM((seq, 16, half_width), BF16),
            pltpu.VMEM((rows, width), BF16),
            pltpu.VMEM((features, rows), F32),
            pltpu.VMEM((BLK, 128), F32),
            pltpu.VMEM((mp, BLK, 128), F32),
            pltpu.VMEM((8, 2 * rows), F32),
            pltpu.VMEM((mp, 8, 2 * rows), F32),
            pltpu.VMEM((2, half, 2, share + 8, rows), jnp.int16),
            pltpu.VMEM((2, half, 2, share + 8, rows), jnp.int16),
            pltpu.VMEM((share + 8, rows), jnp.int16),
            pltpu.VMEM((share + 8, rows), jnp.int16),
            dma((4,)),
            dma((3,)),
            dma, dma, dma, dma, dma, dma, dma, dma,
            dma((2, half, 2)),
            dma((2, half, 2)),
            dma, dma,
        ],
        compiler_params=pltpu.CompilerParams(
            collective_id=0, has_side_effects=True, vmem_limit_bytes=48 * 2**20
        ),
        name="tiles",
    )(
        maps,
        vit_hidden,
        vit_gain.reshape(1, features),
        vit_bias.reshape(1, features),
        proj_weight,
        text_emb,
        llm_gain.reshape(1, width),
        cotangent,
    )
    return (normed, grad_text, grad_vit[:, :share])


def solution(mesh):
    in_specs = (
        P("seq", None),
        P(),
        P(),
        P(None, "mp"),
        P("seq", "mp"),
        P("mp"),
        P("seq", "mp"),
        P(),
        P(),
    )
    out_specs = (P("seq", "mp"), P("seq", "mp"), P("seq", "mp"))
    return jax.shard_map(body, mesh=mesh, in_specs=in_specs, out_specs=out_specs, check_vma=False)
```

```python
import functools

import jax
import jax.numpy as jnp
from jax import lax
from jax.experimental import pallas as pl
from jax.experimental.pallas import tpu as pltpu
from jax.sharding import PartitionSpec as P

BLK = 8
EPSILON = 1e-05
F32 = jnp.float32
BF16 = jnp.bfloat16
MESH = pl.DeviceIdType.MESH
NT = (((1,), (1,)), ((), ()))


def three_parts(x):
    hi = x.astype(BF16).astype(F32)
    mid = (x - hi).astype(BF16).astype(F32)
    return hi, mid, (x - hi) - mid


def stacked(parts, rows, width):
    row = lax.broadcasted_iota(jnp.int32, (rows, width), 0)
    out = jnp.zeros((rows, width), F32)
    for i, part in enumerate(parts):
        out = jnp.where(row == i, jnp.broadcast_to(part, (rows, width)), out)
    return out.astype(BF16)


def folded(x):
    half = x.shape[1] // 2
    return jnp.concatenate([x[:, :half], x[:, half:]], axis=0)


def unfolded(x):
    return jnp.concatenate([x[:BLK], x[BLK:]], axis=1)


def coded(x):
    most = jnp.max(jnp.abs(x), axis=0, keepdims=True)
    exponent = jnp.ceil(jnp.log2(jnp.maximum(most, 1e-30) * 1.0001)) - 15.0
    codes = jnp.clip(jnp.round(x * jnp.exp2(-exponent)), -32767.0, 32767.0)
    below = jnp.broadcast_to(exponent, (8, x.shape[1]))
    return jnp.concatenate([codes, below], axis=0).astype(jnp.int32).astype(jnp.int16)


def decoded(q):
    values = q.astype(jnp.int32).astype(F32)
    rows = q.shape[0] - 8
    return values[:rows] * jnp.exp2(values[rows : rows + 1])


def kernel(
    seq, ny, full_width,
    starts, owners, vit_hbm, gain_hbm, bias_hbm, weight_hbm, text_hbm, llm_hbm, cot_hbm,
    normed_hbm, gtext_hbm, gvit_hbm,
    table, maps, gain_ref, bias_ref, llm_ref,
    vit, weight, text, cot, normed_v, gtext_v, gvit_v,
    nvit, colstat, pre, select, hid,
    out_buf, in_buf, merged, scaled_cot, inv_of, slope_of, back_out, back_even, back_odd,
    gembed, weighted_hi, weighted_lo, partial, kept, turned,
    stat_out, stat_in, stat_zout, stat_zin, mean_out, mean_in, mean_zout, mean_zin,
    ring_out, ring_in, z_out, z_in,
    local_sem, store_sem, a2a_send, a2a_recv, back_send, back_recv,
    sum_send, sum_recv, sum_zsend, sum_zrecv, ring_send, ring_recv, z_send, z_recv,
):
    mp = 2 * ny
    me = lax.axis_index("seq")
    rank = lax.axis_index("mp")
    zh = rank // ny
    y = rank % ny
    rows, features = vit.shape
    width = weight.shape[1]
    tile_blocks = rows // BLK
    local_blocks = text.shape[0] // BLK
    share = features // mp
    half = ny // 2
    half_rows = rows // 2

    barrier = pltpu.get_barrier_semaphore()

    loads = [
        pltpu.make_async_copy(vit_hbm, vit, local_sem.at[0]),
        pltpu.make_async_copy(gain_hbm, gain_ref.at[0], local_sem.at[1]),
        pltpu.make_async_copy(bias_hbm, bias_ref.at[0], local_sem.at[2]),
        pltpu.make_async_copy(weight_hbm, weight, local_sem.at[3]),
        pltpu.make_async_copy(text_hbm, text, local_sem.at[4]),
        pltpu.make_async_copy(cot_hbm, cot, local_sem.at[5]),
        pltpu.make_async_copy(llm_hbm, llm_ref.at[0], local_sem.at[6]),
    ]
    for load in loads:
        load.start()

    def greet_seq(i, carry):
        pl.semaphore_signal(barrier, inc=1, device_id={"seq": lax.rem(me + i, seq)}, device_id_type=MESH)
        return carry

    def greet_mp(i, carry):
        pl.semaphore_signal(barrier, inc=1, device_id={"mp": zh * ny + lax.rem(y + i, ny)}, device_id_type=MESH)
        return carry

    lax.fori_loop(1, seq, greet_seq, 0)
    lax.fori_loop(1, ny, greet_mp, 0)
    other_z = (1 - zh) * ny + y
    pl.semaphore_signal(barrier, inc=1, device_id={"mp": other_z}, device_id_type=MESH)

    lane = lax.broadcasted_iota(jnp.int32, (BLK, 128), 1)

    def look_up(t, found):
        source, start_of = found
        start, owner = starts[t], owners[t]
        away = lax.rem(me - lax.rem(start, seq) + seq, seq)
        hit = (lane == lax.div(start + away, seq)) & (jnp.full((BLK, 128), away, jnp.int32) < tile_blocks)
        return jnp.where(hit, owner, source), jnp.where(lane == owner, start, start_of)

    empty = jnp.zeros((BLK, 128), jnp.int32)
    source, start_of = lax.fori_loop(0, seq, look_up, (empty - 1, empty), unroll=4)
    table[...] = jnp.where(lax.broadcasted_iota(jnp.int32, (BLK, 128), 0) == 0, source, start_of)
    table_copy = pltpu.make_async_copy(table, maps, local_sem.at[7])
    table_copy.start()

    for load in loads[:3]:
        load.wait()
    gain = gain_ref[...]
    bias = bias_ref[...]
    lane16 = lax.broadcasted_iota(jnp.int32, (16, 128), 1)

    def norm_rows(i, carry):
        at = pl.ds(pl.multiple_of(i * 16, 16), 16)
        x = vit[at, :].astype(F32)
        mean = jnp.sum(x, axis=1, keepdims=True) / features
        centred = x - mean
        inv = lax.rsqrt(jnp.sum(centred * centred, axis=1, keepdims=True) / features + EPSILON)
        nvit[at, :] = (centred * inv * gain + bias).astype(BF16)
        colstat[at, :] = jnp.where(lane16 == 0, mean, inv)
        return carry

    lax.fori_loop(0, rows // 16, norm_rows, 0)
    nvit[rows : rows + 16, :] = stacked(three_parts(gain) + three_parts(bias), 16, features)

    loads[3].wait()
    for n in range(2):
        cols = slice(n * (width // 2), (n + 1) * (width // 2))
        product = jnp.dot(nvit[...], weight[:, cols], preferred_element_type=F32)
        pre[:, :, cols] = product.reshape(tile_blocks + 2, BLK, width // 2)

    pl.semaphore_wait(barrier, seq - 1 + ny)

    table_copy.wait()
    own_start = maps[1, me]
    own_phase = lax.rem(own_start, seq)

    def block_for(target):
        block = lax.rem(target - own_phase + seq, seq)
        return folded(pre[jnp.minimum(block, tile_blocks - 1)]).astype(BF16)

    def send_block(i, carry):
        target = lax.rem(me + i, seq)
        out_buf[target] = block_for(target)
        pltpu.make_async_remote_copy(
            src_ref=out_buf.at[target], dst_ref=in_buf.at[me], send_sem=a2a_send, recv_sem=a2a_recv,
            device_id={"seq": target}, device_id_type=MESH,
        ).start()
        return carry

    lax.fori_loop(1, seq, send_block, 0)
    in_buf[me] = block_for(me)

    for load in loads[4:]:
        load.wait()
    llm = llm_ref[...]

    def scale_pair(i, carry):
        at = pl.ds(pl.multiple_of(i * 16, 16), 16)
        scaled_pair = llm * cot[at, :].astype(F32)
        for h in range(2):
            scaled_cot[i * 2 + h] = scaled_pair[h * 8 : h * 8 + 8]
        return carry

    lax.fori_loop(0, local_blocks // 2, scale_pair, 0, unroll=2)
    column = lax.broadcasted_iota(jnp.int32, (16, features), 1)
    within = lax.broadcasted_iota(jnp.int32, (16, features), 0)

    def pick_rows(i, carry):
        hit = column == rank * share + i * 16 + within
        select[pl.ds(pl.multiple_of(i * 16, 16), 16), :] = jnp.where(hit, 1.0, 0.0).astype(BF16)
        return carry

    lax.fori_loop(0, select.shape[0] // 16, pick_rows, 0)
    hid[...] = lax.dot_general(vit[...], select[...], NT, preferred_element_type=F32)
    gains = lax.dot_general(nvit[rows : rows + 16, :], select[...], NT, preferred_element_type=F32)
    gain_row = gains[0:1] + gains[1:2] + gains[2:3]

    waiting = in_buf.at[pl.ds(0, seq - 1)]
    pltpu.make_async_copy(waiting, waiting, a2a_recv).wait()

    def merge_pair(i, sums):
        at = pl.ds(pl.multiple_of(i * 16, 16), 16)
        text_pair = text[at, :].astype(F32)
        for h in range(2):
            b = i * 2 + h
            source = maps[0, b]
            arrived = unfolded(in_buf[jnp.maximum(source, 0)].astype(F32))
            is_image = jnp.full((BLK, width), source, jnp.int32) >= 0
            m = jnp.where(is_image, arrived, text_pair[h * 8 : h * 8 + 8])
            merged[b] = m
            square = jnp.sum(m * m, axis=1, keepdims=True)
            product = jnp.sum(scaled_cot[b] * m, axis=1, keepdims=True)
            sums = jnp.where(lane == b, square, sums)
            sums = jnp.where(lane == b + 64, product, sums)
        return sums

    stat_out[...] = lax.fori_loop(
        0, local_blocks // 2, merge_pair, jnp.ones((BLK, 128), F32), unroll=2
    )

    def start_sum(which, out, into):
        def send(i, carry):
            pltpu.make_async_remote_copy(
                src_ref=out, dst_ref=into.at[y], send_sem=sum_send.at[which], recv_sem=sum_recv.at[which],
                device_id={"mp": zh * ny + lax.rem(y + i, ny)}, device_id_type=MESH,
            ).start()
            return carry

        lax.fori_loop(1, ny, send, 0)
        into[y] = out[...]

    def middle_sum(which, into, zout, zin):
        waiting = into.at[pl.ds(0, ny - 1)]
        pltpu.make_async_copy(waiting, waiting, sum_recv.at[which]).wait()
        total = into[0]
        for i in range(1, ny):
            total = total + into[i]
        zout[...] = total
        copy = pltpu.make_async_remote_copy(
            src_ref=zout, dst_ref=zin, send_sem=sum_zsend.at[which], recv_sem=sum_zrecv.at[which],
            device_id={"mp": other_z}, device_id_type=MESH,
        )
        copy.start()
        return copy

    start_sum(0, stat_out, stat_in)
    stat_copy = middle_sum(0, stat_in, stat_zout, stat_zin)
    stat_copy.wait_recv()
    total = stat_zout[...] + stat_zin[...]
    inv_all = lax.rsqrt(total / full_width + EPSILON)
    slope_all = inv_all * inv_all * inv_all * pltpu.roll(total, 64, 1) / full_width
    for b in range(local_blocks):
        inv_of[b] = jnp.broadcast_to(inv_all[:, b : b + 1], (BLK, 128))
        slope_of[b] = jnp.broadcast_to(slope_all[:, b : b + 1], (BLK, 128))

    def wide(x):
        return jnp.concatenate([x] * (width // 128), axis=1)

    chips = seq // 2
    back_in = (back_even, back_odd)

    def slot_of(device):
        return 2 * (device // 4) + lax.rem(device, 2)

    def send_back(phase):
        core = lax.rem(me // 2 + phase, 2)

        def send(i, carry):
            target = 2 * lax.rem(me // 2 + i, chips) + core
            start = maps[1, target]
            block = start + lax.rem(me - lax.rem(start, seq) + seq, seq)
            b = jnp.minimum(block // seq, local_blocks - 1)
            grad = wide(inv_of[b]) * scaled_cot[b] - merged[b] * wide(slope_of[b])
            value = folded(grad).astype(BF16)

            @pl.when(target == me)
            def _():
                back_in[phase][slot_of(me)] = value

            @pl.when(target != me)
            def _():
                back_out[target] = value
                pltpu.make_async_remote_copy(
                    src_ref=back_out.at[target], dst_ref=back_in[phase].at[slot_of(me)],
                    send_sem=back_send.at[phase], recv_sem=back_recv.at[phase],
                    device_id={"seq": target}, device_id_type=MESH,
                ).start()

            return carry

        lax.fori_loop(0, chips, send, 0)

    send_back(0)

    def norm_pair(i, carry):
        at = pl.ds(pl.multiple_of(i * 16, 16), 16)
        normed_pair, text_pair = [], []
        for h in range(2):
            b = i * 2 + h
            inv = wide(inv_of[b])
            m = merged[b]
            normed_pair.append(m * inv * llm)
            grad = inv * scaled_cot[b] - m * wide(slope_of[b])
            is_image = jnp.full((BLK, width), maps[0, b], jnp.int32) >= 0
            text_pair.append(jnp.where(is_image, 0.0, grad))
        normed_v[at, :] = jnp.concatenate(normed_pair, axis=0).astype(BF16)
        gtext_v[at, :] = jnp.concatenate(text_pair, axis=0).astype(BF16)
        return carry

    lax.fori_loop(0, local_blocks // 2, norm_pair, 0, unroll=2)
    stores = [
        pltpu.make_async_copy(normed_v, normed_hbm, store_sem.at[0]),
        pltpu.make_async_copy(gtext_v, gtext_hbm, store_sem.at[1]),
    ]
    for store in stores:
        store.start()

    below = pre[tile_blocks]
    gain_weight = below[0:1] + below[1:2] + below[2:3]
    bias_weight = below[3:4] + below[4:5] + below[5:6]
    gain_parts = stacked(three_parts(gain_weight), 16, width)
    ones = jnp.ones((16, width), BF16)

    def wait_phase(buffer, sem, phase):
        own_in = lax.rem(me // 2 + me, 2) == phase

        @pl.when(own_in)
        def _():
            waiting = buffer.at[pl.ds(0, chips - 1)]
            pltpu.make_async_copy(waiting, waiting, sem.at[phase]).wait()

        @pl.when(jnp.logical_not(own_in))
        def _():
            waiting = buffer.at[pl.ds(0, chips)]
            pltpu.make_async_copy(waiting, waiting, sem.at[phase]).wait()

    def receive(phase):
        wait_phase(back_in[phase], back_recv, phase)
        parity = lax.rem(me + phase, 2)

        def gather_pair(i, carry):
            pair, embed = [], []
            for c in range(2):
                j = lax.rem(2 * parity + c - lax.rem(own_phase, 4) + 4, 4) + 4 * i
                device = lax.rem(own_phase + j, seq)
                pair.append(unfolded(back_in[phase][slot_of(device)].astype(F32)))
                embed.append(pre[j])
            at = pl.ds(pl.multiple_of(i * 16, 16), 16)
            g = jnp.concatenate(pair, axis=0)
            weighted = g * (jnp.concatenate(embed, axis=0) - bias_weight)
            high = weighted.astype(BF16)
            gembed[phase, at, :] = g.astype(BF16)
            weighted_hi[phase, at, :] = high
            weighted_lo[phase, at, :] = (weighted - high.astype(F32)).astype(BF16)
            return carry

        lax.fori_loop(0, tile_blocks // 4, gather_pair, 0)
        g = gembed[phase]
        step_rows = features // 8
        for n in range(8):
            piece = slice(n * step_rows, (n + 1) * step_rows)
            partial[phase, piece, :] = lax.dot_general(
                weight[piece, :], g, NT, preferred_element_type=F32
            )

    def two_sums(phase):
        first = lax.dot_general(gain_parts, gembed[phase], NT, preferred_element_type=F32)
        second = lax.dot_general(ones, weighted_hi[phase], NT, preferred_element_type=F32)
        second = second + lax.dot_general(ones, weighted_lo[phase], NT, preferred_element_type=F32)
        return jnp.sum(first, axis=0, keepdims=True), second[0:1]

    def own(phase, target, h):
        start = ((1 - zh if h == 0 else zh) * ny + target) * share
        return partial[phase, pl.ds(pl.multiple_of(start, 8), share), :]

    def ring_copy(phase, direction, step, h):
        to = lax.rem(y + 1, ny) if direction == 0 else lax.rem(y + ny - 1, ny)
        at = (phase, direction, step, h)
        return pltpu.make_async_remote_copy(
            src_ref=ring_out.at[at], dst_ref=ring_in.at[at],
            send_sem=ring_send.at[at], recv_sem=ring_recv.at[at],
            device_id={"mp": zh * ny + to}, device_id_type=MESH,
        )

    copies = []

    def ring_step(phase, step):
        for h in range(2):
            for direction in range(2):
                if step == 0 and h != direction:
                    continue
                away = half - step
                target = lax.rem(y + away, ny) if direction == 0 else lax.rem(y + ny - away, ny)
                value = own(phase, target, h)
                if step >= 2 or (step == 1 and h == direction):
                    ring_copy(phase, direction, step - 1, h).wait_recv()
                    value = value + decoded(ring_in[phase, direction, step - 1, h])
                ring_out[phase, direction, step, h] = coded(value)
                copy = ring_copy(phase, direction, step, h)
                copy.start()
                copies.append(copy)

    def chain_end(phase, h):
        value = own(phase, y, h)
        for direction in range(2):
            if half >= 2 or h == direction:
                ring_copy(phase, direction, half - 1, h).wait_recv()
                value = value + decoded(ring_in[phase, direction, half - 1, h])
        return value

    def start_z(phase):
        z_out[phase] = coded(chain_end(phase, 0))
        copy = pltpu.make_async_remote_copy(
            src_ref=z_out.at[phase], dst_ref=z_in.at[phase],
            send_sem=z_send.at[phase], recv_sem=z_recv.at[phase],
            device_id={"mp": other_z}, device_id_type=MESH,
        )
        copy.start()
        copies.append(copy)
        kept[phase] = chain_end(phase, 1)
        return copy

    wait_phase(back_out, back_send, 0)
    send_back(1)
    receive(0)
    early = half // 2
    for step in range(early):
        ring_step(0, step)
    receive(1)
    for step in range(early, half):
        ring_step(0, step)
        ring_step(1, step - early)
        if step == early:
            sums = [two_sums(0), two_sums(1)]
            mean_out[...] = jnp.concatenate(
                [sums[0][0], sums[1][0], sums[0][1], sums[1][1], jnp.zeros((4, half_rows), F32)], axis=0
            )
            start_sum(1, mean_out, mean_in)
    mean_copy = middle_sum(1, mean_in, mean_zout, mean_zin)
    z_copies = [start_z(0)]
    for step in range(half - early, half):
        ring_step(1, step)
    z_copies.append(start_z(1))

    mean_copy.wait_recv()
    means = (mean_zout[...] + mean_zin[...]) / features
    for phase in range(2):
        z_copies[phase].wait_recv()
        value = kept[phase] + decoded(z_in[phase])
        lines = [value, means[phase : phase + 1], means[phase + 2 : phase + 3]]
        lines.append(jnp.zeros((gvit_v.shape[1] - share - 2, half_rows), F32))
        turn = jnp.transpose(jnp.concatenate(lines, axis=0))
        at = slice(phase * (tile_blocks // 2), (phase + 1) * (tile_blocks // 2))
        turned[at] = turn.reshape(tile_blocks // 2, BLK, gvit_v.shape[1])

    def finish_pair(i, carry):
        at = pl.ds(pl.multiple_of(i * 16, 16), 16)
        pair = []
        for c in range(2):
            j = i * 2 + c
            device = own_phase + j
            phase = lax.rem(device // 2 + me, 2)
            pair.append(turned[phase * (tile_blocks // 2) + 2 * (j // 4) + lax.rem(device, 2)])
        value = jnp.concatenate(pair, axis=0)
        inv = colstat[at, 1:2]
        unit = (hid[at, :] - colstat[at, 0:1]) * inv
        first = value[:, share : share + 1]
        second = value[:, share + 1 : share + 2]
        gvit_v[at, :] = (inv * (value * gain_row - first - unit * second)).astype(BF16)
        return carry

    lax.fori_loop(0, tile_blocks // 2, finish_pair, 0, unroll=2)
    last = pltpu.make_async_copy(gvit_v, gvit_hbm, store_sem.at[2])
    last.start()

    waiting = out_buf.at[pl.ds(0, seq - 1)]
    pltpu.make_async_copy(waiting, waiting, a2a_send).wait()
    wait_phase(back_out, back_send, 1)
    for which, into, copy in ((0, stat_in, stat_copy), (1, mean_in, mean_copy)):
        waiting = into.at[pl.ds(0, ny - 1)]
        pltpu.make_async_copy(waiting, waiting, sum_send.at[which]).wait()
        copy.wait_send()
    for copy in copies:
        copy.wait_send()
    for store in stores:
        store.wait()
    last.wait()


def body(
    vit_hidden,
    vit_gain,
    vit_bias,
    proj_weight,
    text_emb,
    llm_gain,
    cotangent,
    tile_start,
    tile_owner,
):
    seq = lax.axis_size("seq")
    mp = lax.axis_size("mp")
    ny = mp // 2
    rows, features = vit_hidden.shape
    width = proj_weight.shape[1]
    tokens = text_emb.shape[0]
    tile_blocks = rows // BLK
    local_blocks = tokens // BLK
    share = features // mp
    padded = -(-share // 128) * 128

    anywhere = pl.BlockSpec(memory_space=pl.ANY)
    half_width = width // 2
    half = ny // 2
    dma = pltpu.SemaphoreType.DMA
    normed, grad_text, grad_vit = pl.pallas_call(
        functools.partial(kernel, seq, ny, width * mp),
        out_shape=(
            jax.ShapeDtypeStruct((tokens, width), BF16),
            jax.ShapeDtypeStruct((tokens, width), BF16),
            jax.ShapeDtypeStruct((rows, padded), BF16),
        ),
        in_specs=[pl.BlockSpec(memory_space=pltpu.SMEM)] * 2 + [anywhere] * 7,
        out_specs=(anywhere, anywhere, anywhere),
        scratch_shapes=[
            pltpu.VMEM((BLK, 128), jnp.int32),
            pltpu.SMEM((BLK, 128), jnp.int32),
            pltpu.VMEM((1, features), F32),
            pltpu.VMEM((1, features), F32),
            pltpu.VMEM((1, width), F32),
            pltpu.VMEM((rows, features), BF16),
            pltpu.VMEM((features, width), BF16),
            pltpu.VMEM((tokens, width), BF16),
            pltpu.VMEM((tokens, width), BF16),
            pltpu.VMEM((tokens, width), BF16),
            pltpu.VMEM((tokens, width), BF16),
            pltpu.VMEM((rows, padded), BF16),
            pltpu.VMEM((rows + 16, features), BF16),
            pltpu.VMEM((rows, 128), F32),
            pltpu.VMEM((tile_blocks + 2, BLK, width), F32),
            pltpu.VMEM((padded, features), BF16),
            pltpu.VMEM((rows, padded), F32),
            pltpu.VMEM((seq, 16, half_width), BF16),
            pltpu.VMEM((seq, 16, half_width), BF16),
            pltpu.VMEM((local_blocks, BLK, width), F32),
            pltpu.VMEM((local_blocks, BLK, width), F32),
            pltpu.VMEM((local_blocks, BLK, 128), F32),
            pltpu.VMEM((local_blocks, BLK, 128), F32),
            pltpu.VMEM((seq, 16, half_width), BF16),
            pltpu.VMEM((seq // 2, 16, half_width), BF16),
            pltpu.VMEM((seq // 2, 16, half_width), BF16),
            pltpu.VMEM((2, rows // 2, width), BF16),
            pltpu.VMEM((2, rows // 2, width), BF16),
            pltpu.VMEM((2, rows // 2, width), BF16),
            pltpu.VMEM((2, features, rows // 2), F32),
            pltpu.VMEM((2, share, rows // 2), F32),
            pltpu.VMEM((tile_blocks, BLK, padded), F32),
            pltpu.VMEM((BLK, 128), F32),
            pltpu.VMEM((ny, BLK, 128), F32),
            pltpu.VMEM((BLK, 128), F32),
            pltpu.VMEM((BLK, 128), F32),
            pltpu.VMEM((8, rows // 2), F32),
            pltpu.VMEM((ny, 8, rows // 2), F32),
            pltpu.VMEM((8, rows // 2), F32),
            pltpu.VMEM((8, rows // 2), F32),
            pltpu.VMEM((2, 2, half, 2, share + 8, rows // 2), jnp.int16),
            pltpu.VMEM((2, 2, half, 2, share + 8, rows // 2), jnp.int16),
            pltpu.VMEM((2, share + 8, rows // 2), jnp.int16),
            pltpu.VMEM((2, share + 8, rows // 2), jnp.int16),
            dma((8,)),
            dma((3,)),
            dma, dma, dma((2,)), dma((2,)),
            dma((2,)), dma((2,)), dma((2,)), dma((2,)),
            dma((2, 2, half, 2)), dma((2, 2, half, 2)),
            dma((2,)), dma((2,)),
        ],
        compiler_params=pltpu.CompilerParams(
            collective_id=0, has_side_effects=True, vmem_limit_bytes=60 * 2**20
        ),
        name="tiles",
    )(
        tile_start,
        tile_owner,
        vit_hidden,
        vit_gain,
        vit_bias,
        proj_weight,
        text_emb,
        llm_gain,
        cotangent,
    )
    return (normed, grad_text, grad_vit[:, :share])


def solution(mesh):
    in_specs = (
        P("seq", None),
        P(),
        P(),
        P(None, "mp"),
        P("seq", "mp"),
        P("mp"),
        P("seq", "mp"),
        P(),
        P(),
    )
    out_specs = (P("seq", "mp"), P("seq", "mp"), P("seq", "mp"))
    return jax.shard_map(body, mesh=mesh, in_specs=in_specs, out_specs=out_specs, check_vma=False)
```

```python
import functools

import jax
import jax.numpy as jnp
from jax import lax
from jax.experimental import pallas as pl
from jax.experimental.pallas import tpu as pltpu
from jax.sharding import PartitionSpec as P

BLK = 8
EPSILON = 1e-05
F32 = jnp.float32
BF16 = jnp.bfloat16
MESH = pl.DeviceIdType.MESH
NT = (((1,), (1,)), ((), ()))


def three_parts(x):
    hi = x.astype(BF16).astype(F32)
    mid = (x - hi).astype(BF16).astype(F32)
    return hi, mid, (x - hi) - mid


def stacked(parts, rows, width):
    row = lax.broadcasted_iota(jnp.int32, (rows, width), 0)
    out = jnp.zeros((rows, width), F32)
    for i, part in enumerate(parts):
        out = jnp.where(row == i, jnp.broadcast_to(part, (rows, width)), out)
    return out.astype(BF16)


def folded(x):
    half = x.shape[1] // 2
    return jnp.concatenate([x[:, :half], x[:, half:]], axis=0)


def unfolded(x):
    return jnp.concatenate([x[:BLK], x[BLK:]], axis=1)


def coded(x):
    most = jnp.max(jnp.abs(x), axis=0, keepdims=True)
    exponent = jnp.ceil(jnp.log2(jnp.maximum(most, 1e-30) * 1.0001)) - 15.0
    codes = jnp.clip(jnp.round(x * jnp.exp2(-exponent)), -32767.0, 32767.0)
    below = jnp.broadcast_to(exponent, (8, x.shape[1]))
    return jnp.concatenate([codes, below], axis=0).astype(jnp.int32).astype(jnp.int16)


def decoded(q):
    values = q.astype(jnp.int32).astype(F32)
    rows = q.shape[0] - 8
    return values[:rows] * jnp.exp2(values[rows : rows + 1])


def kernel(
    seq, ny, full_width,
    starts, owners, vit_hbm, gain_hbm, bias_hbm, weight_hbm, text_hbm, llm_hbm, cot_hbm,
    normed_hbm, gtext_hbm, gvit_hbm,
    table, maps, gain_ref, bias_ref, llm_ref,
    vit, weight, text, cot, normed_v, gtext_v, gvit_v,
    nvit, colstat, pre, select, hid,
    out_buf, in_buf, merged, scaled_cot, inv_of, slope_of, back_out, back_even, back_odd,
    gembed, weighted_hi, weighted_lo, partial, kept, turned,
    stat_out, stat_in, stat_zout, stat_zin, mean_out, mean_in, mean_zout, mean_zin,
    ring_out, ring_in, z_out, z_in,
    local_sem, store_sem, a2a_send, a2a_recv, back_send, back_recv,
    sum_send, sum_recv, sum_zsend, sum_zrecv, ring_send, ring_recv, z_send, z_recv,
):
    mp = 2 * ny
    me = lax.axis_index("seq")
    rank = lax.axis_index("mp")
    zh = rank // ny
    y = rank % ny
    rows, features = vit.shape
    width = weight.shape[1]
    tile_blocks = rows // BLK
    local_blocks = text.shape[0] // BLK
    share = features // mp
    half = ny // 2
    half_rows = rows // 2

    barrier = pltpu.get_barrier_semaphore()

    loads = [
        pltpu.make_async_copy(vit_hbm, vit, local_sem.at[0]),
        pltpu.make_async_copy(gain_hbm, gain_ref.at[0], local_sem.at[1]),
        pltpu.make_async_copy(bias_hbm, bias_ref.at[0], local_sem.at[2]),
        pltpu.make_async_copy(weight_hbm, weight, local_sem.at[3]),
        pltpu.make_async_copy(text_hbm, text, local_sem.at[4]),
        pltpu.make_async_copy(cot_hbm, cot, local_sem.at[5]),
        pltpu.make_async_copy(llm_hbm, llm_ref.at[0], local_sem.at[6]),
    ]
    for load in loads:
        load.start()

    def greet_seq(i, carry):
        pl.semaphore_signal(barrier, inc=1, device_id={"seq": lax.rem(me + i, seq)}, device_id_type=MESH)
        return carry

    def greet_mp(i, carry):
        pl.semaphore_signal(barrier, inc=1, device_id={"mp": zh * ny + lax.rem(y + i, ny)}, device_id_type=MESH)
        return carry

    lax.fori_loop(1, seq, greet_seq, 0)
    lax.fori_loop(1, ny, greet_mp, 0)
    other_z = (1 - zh) * ny + y
    pl.semaphore_signal(barrier, inc=1, device_id={"mp": other_z}, device_id_type=MESH)

    lane = lax.broadcasted_iota(jnp.int32, (BLK, 128), 1)

    def look_up(t, found):
        source, start_of = found
        start, owner = starts[t], owners[t]
        away = lax.rem(me - lax.rem(start, seq) + seq, seq)
        hit = (lane == lax.div(start + away, seq)) & (jnp.full((BLK, 128), away, jnp.int32) < tile_blocks)
        return jnp.where(hit, owner, source), jnp.where(lane == owner, start, start_of)

    empty = jnp.zeros((BLK, 128), jnp.int32)
    source, start_of = lax.fori_loop(0, seq, look_up, (empty - 1, empty), unroll=4)
    table[...] = jnp.where(lax.broadcasted_iota(jnp.int32, (BLK, 128), 0) == 0, source, start_of)
    table_copy = pltpu.make_async_copy(table, maps, local_sem.at[7])
    table_copy.start()

    for load in loads[:3]:
        load.wait()
    gain = gain_ref[...]
    bias = bias_ref[...]
    lane16 = lax.broadcasted_iota(jnp.int32, (16, 128), 1)

    def norm_rows(i, carry):
        at = pl.ds(pl.multiple_of(i * 16, 16), 16)
        x = vit[at, :].astype(F32)
        mean = jnp.sum(x, axis=1, keepdims=True) / features
        centred = x - mean
        inv = lax.rsqrt(jnp.sum(centred * centred, axis=1, keepdims=True) / features + EPSILON)
        nvit[at, :] = (centred * inv * gain + bias).astype(BF16)
        colstat[at, :] = jnp.where(lane16 == 0, mean, inv)
        return carry

    lax.fori_loop(0, rows // 16, norm_rows, 0)
    nvit[rows : rows + 16, :] = stacked(three_parts(gain) + three_parts(bias), 16, features)

    loads[3].wait()
    for n in range(2):
        cols = slice(n * (width // 2), (n + 1) * (width // 2))
        product = jnp.dot(nvit[...], weight[:, cols], preferred_element_type=F32)
        pre[:, :, cols] = product.reshape(tile_blocks + 2, BLK, width // 2)

    pl.semaphore_wait(barrier, seq - 1 + ny)

    table_copy.wait()
    own_start = maps[1, me]
    own_phase = lax.rem(own_start, seq)

    def block_for(target):
        block = lax.rem(target - own_phase + seq, seq)
        return folded(pre[jnp.minimum(block, tile_blocks - 1)]).astype(BF16)

    def send_block(i, carry):
        target = lax.rem(me + i, seq)
        out_buf[target] = block_for(target)
        pltpu.make_async_remote_copy(
            src_ref=out_buf.at[target], dst_ref=in_buf.at[me], send_sem=a2a_send, recv_sem=a2a_recv,
            device_id={"seq": target}, device_id_type=MESH,
        ).start()
        return carry

    lax.fori_loop(1, seq, send_block, 0)
    in_buf[me] = block_for(me)

    for load in loads[4:]:
        load.wait()
    llm = llm_ref[...]

    def scale_pair(i, carry):
        at = pl.ds(pl.multiple_of(i * 16, 16), 16)
        scaled_pair = llm * cot[at, :].astype(F32)
        for h in range(2):
            scaled_cot[i * 2 + h] = scaled_pair[h * 8 : h * 8 + 8]
        return carry

    lax.fori_loop(0, local_blocks // 2, scale_pair, 0, unroll=2)
    column = lax.broadcasted_iota(jnp.int32, (16, features), 1)
    within = lax.broadcasted_iota(jnp.int32, (16, features), 0)

    def pick_rows(i, carry):
        hit = column == rank * share + i * 16 + within
        select[pl.ds(pl.multiple_of(i * 16, 16), 16), :] = jnp.where(hit, 1.0, 0.0).astype(BF16)
        return carry

    lax.fori_loop(0, select.shape[0] // 16, pick_rows, 0)
    hid[...] = lax.dot_general(vit[...], select[...], NT, preferred_element_type=F32)
    gains = lax.dot_general(nvit[rows : rows + 16, :], select[...], NT, preferred_element_type=F32)
    gain_row = gains[0:1] + gains[1:2] + gains[2:3]

    waiting = in_buf.at[pl.ds(0, seq - 1)]
    pltpu.make_async_copy(waiting, waiting, a2a_recv).wait()

    def merge_pair(i, sums):
        at = pl.ds(pl.multiple_of(i * 16, 16), 16)
        text_pair = text[at, :].astype(F32)
        for h in range(2):
            b = i * 2 + h
            source = maps[0, b]
            arrived = unfolded(in_buf[jnp.maximum(source, 0)].astype(F32))
            is_image = jnp.full((BLK, width), source, jnp.int32) >= 0
            m = jnp.where(is_image, arrived, text_pair[h * 8 : h * 8 + 8])
            merged[b] = m
            square = jnp.sum(m * m, axis=1, keepdims=True)
            product = jnp.sum(scaled_cot[b] * m, axis=1, keepdims=True)
            sums = jnp.where(lane == b, square, sums)
            sums = jnp.where(lane == b + 64, product, sums)
        return sums

    stat_out[...] = lax.fori_loop(
        0, local_blocks // 2, merge_pair, jnp.ones((BLK, 128), F32), unroll=2
    )

    def start_sum(which, out, into):
        def send(i, carry):
            pltpu.make_async_remote_copy(
                src_ref=out, dst_ref=into.at[y], send_sem=sum_send.at[which], recv_sem=sum_recv.at[which],
                device_id={"mp": zh * ny + lax.rem(y + i, ny)}, device_id_type=MESH,
            ).start()
            return carry

        lax.fori_loop(1, ny, send, 0)
        into[y] = out[...]

    def middle_sum(which, into, zout, zin):
        waiting = into.at[pl.ds(0, ny - 1)]
        pltpu.make_async_copy(waiting, waiting, sum_recv.at[which]).wait()
        total = into[0]
        for i in range(1, ny):
            total = total + into[i]
        zout[...] = total
        copy = pltpu.make_async_remote_copy(
            src_ref=zout, dst_ref=zin, send_sem=sum_zsend.at[which], recv_sem=sum_zrecv.at[which],
            device_id={"mp": other_z}, device_id_type=MESH,
        )
        copy.start()
        return copy

    start_sum(0, stat_out, stat_in)
    stat_copy = middle_sum(0, stat_in, stat_zout, stat_zin)
    stat_copy.wait_recv()
    total = stat_zout[...] + stat_zin[...]
    inv_all = lax.rsqrt(total / full_width + EPSILON)
    slope_all = inv_all * inv_all * inv_all * pltpu.roll(total, 64, 1) / full_width
    for b in range(local_blocks):
        inv_of[b] = jnp.broadcast_to(inv_all[:, b : b + 1], (BLK, 128))
        slope_of[b] = jnp.broadcast_to(slope_all[:, b : b + 1], (BLK, 128))

    def wide(x):
        return jnp.concatenate([x] * (width // 128), axis=1)

    chips = seq // 2
    back_in = (back_even, back_odd)

    def slot_of(device):
        return 2 * (device // 4) + lax.rem(device, 2)

    def send_back(phase):
        core = lax.rem(me // 2 + phase, 2)

        def send(i, carry):
            target = 2 * lax.rem(me // 2 + i, chips) + core
            start = maps[1, target]
            block = start + lax.rem(me - lax.rem(start, seq) + seq, seq)
            b = jnp.minimum(block // seq, local_blocks - 1)
            grad = wide(inv_of[b]) * scaled_cot[b] - merged[b] * wide(slope_of[b])
            value = folded(grad).astype(BF16)

            @pl.when(target == me)
            def _():
                back_in[phase][slot_of(me)] = value

            @pl.when(target != me)
            def _():
                back_out[target] = value
                pltpu.make_async_remote_copy(
                    src_ref=back_out.at[target], dst_ref=back_in[phase].at[slot_of(me)],
                    send_sem=back_send.at[phase], recv_sem=back_recv.at[phase],
                    device_id={"seq": target}, device_id_type=MESH,
                ).start()

            return carry

        lax.fori_loop(0, chips, send, 0)

    send_back(0)

    def norm_pair(i, carry):
        at = pl.ds(pl.multiple_of(i * 16, 16), 16)
        normed_pair, text_pair = [], []
        for h in range(2):
            b = i * 2 + h
            inv = wide(inv_of[b])
            m = merged[b]
            normed_pair.append(m * inv * llm)
            grad = inv * scaled_cot[b] - m * wide(slope_of[b])
            is_image = jnp.full((BLK, width), maps[0, b], jnp.int32) >= 0
            text_pair.append(jnp.where(is_image, 0.0, grad))
        normed_v[at, :] = jnp.concatenate(normed_pair, axis=0).astype(BF16)
        gtext_v[at, :] = jnp.concatenate(text_pair, axis=0).astype(BF16)
        return carry

    lax.fori_loop(0, local_blocks // 2, norm_pair, 0, unroll=2)
    stores = [
        pltpu.make_async_copy(normed_v, normed_hbm, store_sem.at[0]),
        pltpu.make_async_copy(gtext_v, gtext_hbm, store_sem.at[1]),
    ]
    for store in stores:
        store.start()

    below = pre[tile_blocks]
    gain_weight = below[0:1] + below[1:2] + below[2:3]
    bias_weight = below[3:4] + below[4:5] + below[5:6]
    gain_parts = stacked(three_parts(gain_weight), 16, width)
    ones = jnp.ones((16, width), BF16)

    def wait_phase(buffer, sem, phase):
        own_in = lax.rem(me // 2 + me, 2) == phase

        @pl.when(own_in)
        def _():
            waiting = buffer.at[pl.ds(0, chips - 1)]
            pltpu.make_async_copy(waiting, waiting, sem.at[phase]).wait()

        @pl.when(jnp.logical_not(own_in))
        def _():
            waiting = buffer.at[pl.ds(0, chips)]
            pltpu.make_async_copy(waiting, waiting, sem.at[phase]).wait()

    def receive(phase):
        wait_phase(back_in[phase], back_recv, phase)
        parity = lax.rem(me + phase, 2)

        def gather_pair(i, carry):
            pair, embed = [], []
            for c in range(2):
                j = lax.rem(2 * parity + c - lax.rem(own_phase, 4) + 4, 4) + 4 * i
                device = lax.rem(own_phase + j, seq)
                pair.append(unfolded(back_in[phase][slot_of(device)].astype(F32)))
                embed.append(pre[j])
            at = pl.ds(pl.multiple_of(i * 16, 16), 16)
            g = jnp.concatenate(pair, axis=0)
            weighted = g * (jnp.concatenate(embed, axis=0) - bias_weight)
            high = weighted.astype(BF16)
            gembed[phase, at, :] = g.astype(BF16)
            weighted_hi[phase, at, :] = high
            weighted_lo[phase, at, :] = (weighted - high.astype(F32)).astype(BF16)
            return carry

        lax.fori_loop(0, tile_blocks // 4, gather_pair, 0)
        g = gembed[phase]
        step_rows = features // 8
        for n in range(8):
            piece = slice(n * step_rows, (n + 1) * step_rows)
            partial[phase, piece, :] = lax.dot_general(
                weight[piece, :], g, NT, preferred_element_type=F32
            )

    def two_sums(phase):
        first = lax.dot_general(gain_parts, gembed[phase], NT, preferred_element_type=F32)
        second = lax.dot_general(ones, weighted_hi[phase], NT, preferred_element_type=F32)
        second = second + lax.dot_general(ones, weighted_lo[phase], NT, preferred_element_type=F32)
        return jnp.sum(first, axis=0, keepdims=True), second[0:1]

    def own(phase, target, h):
        start = ((1 - zh if h == 0 else zh) * ny + target) * share
        return partial[phase, pl.ds(pl.multiple_of(start, 8), share), :]

    def ring_copy(phase, direction, step, h):
        to = lax.rem(y + 1, ny) if direction == 0 else lax.rem(y + ny - 1, ny)
        at = (phase, direction, step, h)
        return pltpu.make_async_remote_copy(
            src_ref=ring_out.at[at], dst_ref=ring_in.at[at],
            send_sem=ring_send.at[at], recv_sem=ring_recv.at[at],
            device_id={"mp": zh * ny + to}, device_id_type=MESH,
        )

    copies = []

    def ring_step(phase, step):
        for h in range(2):
            for direction in range(2):
                if step == 0 and h != direction:
                    continue
                away = half - step
                target = lax.rem(y + away, ny) if direction == 0 else lax.rem(y + ny - away, ny)
                value = own(phase, target, h)
                if step >= 2 or (step == 1 and h == direction):
                    ring_copy(phase, direction, step - 1, h).wait_recv()
                    value = value + decoded(ring_in[phase, direction, step - 1, h])
                ring_out[phase, direction, step, h] = coded(value)
                copy = ring_copy(phase, direction, step, h)
                copy.start()
                copies.append(copy)

    def chain_end(phase, h):
        value = own(phase, y, h)
        for direction in range(2):
            if half >= 2 or h == direction:
                ring_copy(phase, direction, half - 1, h).wait_recv()
                value = value + decoded(ring_in[phase, direction, half - 1, h])
        return value

    def start_z(phase):
        z_out[phase] = coded(chain_end(phase, 0))
        copy = pltpu.make_async_remote_copy(
            src_ref=z_out.at[phase], dst_ref=z_in.at[phase],
            send_sem=z_send.at[phase], recv_sem=z_recv.at[phase],
            device_id={"mp": other_z}, device_id_type=MESH,
        )
        copy.start()
        copies.append(copy)
        kept[phase] = chain_end(phase, 1)
        return copy

    wait_phase(back_out, back_send, 0)
    send_back(1)
    receive(0)
    early = max(1, half - 1)
    for step in range(early):
        ring_step(0, step)
    receive(1)
    for step in range(early, half):
        ring_step(0, step)
        ring_step(1, step - early)
        if step == early:
            sums = [two_sums(0), two_sums(1)]
            mean_out[...] = jnp.concatenate(
                [sums[0][0], sums[1][0], sums[0][1], sums[1][1], jnp.zeros((4, half_rows), F32)], axis=0
            )
            start_sum(1, mean_out, mean_in)
    mean_copy = middle_sum(1, mean_in, mean_zout, mean_zin)
    z_copies = [start_z(0)]
    for step in range(half - early, half):
        ring_step(1, step)
    z_copies.append(start_z(1))

    mean_copy.wait_recv()
    means = (mean_zout[...] + mean_zin[...]) / features
    for phase in range(2):
        z_copies[phase].wait_recv()
        value = kept[phase] + decoded(z_in[phase])
        lines = [value, means[phase : phase + 1], means[phase + 2 : phase + 3]]
        lines.append(jnp.zeros((gvit_v.shape[1] - share - 2, half_rows), F32))
        turn = jnp.transpose(jnp.concatenate(lines, axis=0))
        at = slice(phase * (tile_blocks // 2), (phase + 1) * (tile_blocks // 2))
        turned[at] = turn.reshape(tile_blocks // 2, BLK, gvit_v.shape[1])

    def finish_pair(i, carry):
        at = pl.ds(pl.multiple_of(i * 16, 16), 16)
        pair = []
        for c in range(2):
            j = i * 2 + c
            device = own_phase + j
            phase = lax.rem(device // 2 + me, 2)
            pair.append(turned[phase * (tile_blocks // 2) + 2 * (j // 4) + lax.rem(device, 2)])
        value = jnp.concatenate(pair, axis=0)
        inv = colstat[at, 1:2]
        unit = (hid[at, :] - colstat[at, 0:1]) * inv
        first = value[:, share : share + 1]
        second = value[:, share + 1 : share + 2]
        gvit_v[at, :] = (inv * (value * gain_row - first - unit * second)).astype(BF16)
        return carry

    lax.fori_loop(0, tile_blocks // 2, finish_pair, 0, unroll=2)
    last = pltpu.make_async_copy(gvit_v, gvit_hbm, store_sem.at[2])
    last.start()

    waiting = out_buf.at[pl.ds(0, seq - 1)]
    pltpu.make_async_copy(waiting, waiting, a2a_send).wait()
    wait_phase(back_out, back_send, 1)
    for which, into, copy in ((0, stat_in, stat_copy), (1, mean_in, mean_copy)):
        waiting = into.at[pl.ds(0, ny - 1)]
        pltpu.make_async_copy(waiting, waiting, sum_send.at[which]).wait()
        copy.wait_send()
    for copy in copies:
        copy.wait_send()
    for store in stores:
        store.wait()
    last.wait()


def body(
    vit_hidden,
    vit_gain,
    vit_bias,
    proj_weight,
    text_emb,
    llm_gain,
    cotangent,
    tile_start,
    tile_owner,
):
    seq = lax.axis_size("seq")
    mp = lax.axis_size("mp")
    ny = mp // 2
    rows, features = vit_hidden.shape
    width = proj_weight.shape[1]
    tokens = text_emb.shape[0]
    tile_blocks = rows // BLK
    local_blocks = tokens // BLK
    share = features // mp
    padded = -(-share // 128) * 128

    anywhere = pl.BlockSpec(memory_space=pl.ANY)
    half_width = width // 2
    half = ny // 2
    dma = pltpu.SemaphoreType.DMA
    normed, grad_text, grad_vit = pl.pallas_call(
        functools.partial(kernel, seq, ny, width * mp),
        out_shape=(
            jax.ShapeDtypeStruct((tokens, width), BF16),
            jax.ShapeDtypeStruct((tokens, width), BF16),
            jax.ShapeDtypeStruct((rows, padded), BF16),
        ),
        in_specs=[pl.BlockSpec(memory_space=pltpu.SMEM)] * 2 + [anywhere] * 7,
        out_specs=(anywhere, anywhere, anywhere),
        scratch_shapes=[
            pltpu.VMEM((BLK, 128), jnp.int32),
            pltpu.SMEM((BLK, 128), jnp.int32),
            pltpu.VMEM((1, features), F32),
            pltpu.VMEM((1, features), F32),
            pltpu.VMEM((1, width), F32),
            pltpu.VMEM((rows, features), BF16),
            pltpu.VMEM((features, width), BF16),
            pltpu.VMEM((tokens, width), BF16),
            pltpu.VMEM((tokens, width), BF16),
            pltpu.VMEM((tokens, width), BF16),
            pltpu.VMEM((tokens, width), BF16),
            pltpu.VMEM((rows, padded), BF16),
            pltpu.VMEM((rows + 16, features), BF16),
            pltpu.VMEM((rows, 128), F32),
            pltpu.VMEM((tile_blocks + 2, BLK, width), F32),
            pltpu.VMEM((padded, features), BF16),
            pltpu.VMEM((rows, padded), F32),
            pltpu.VMEM((seq, 16, half_width), BF16),
            pltpu.VMEM((seq, 16, half_width), BF16),
            pltpu.VMEM((local_blocks, BLK, width), F32),
            pltpu.VMEM((local_blocks, BLK, width), F32),
            pltpu.VMEM((local_blocks, BLK, 128), F32),
            pltpu.VMEM((local_blocks, BLK, 128), F32),
            pltpu.VMEM((seq, 16, half_width), BF16),
            pltpu.VMEM((seq // 2, 16, half_width), BF16),
            pltpu.VMEM((seq // 2, 16, half_width), BF16),
            pltpu.VMEM((2, rows // 2, width), BF16),
            pltpu.VMEM((2, rows // 2, width), BF16),
            pltpu.VMEM((2, rows // 2, width), BF16),
            pltpu.VMEM((2, features, rows // 2), F32),
            pltpu.VMEM((2, share, rows // 2), F32),
            pltpu.VMEM((tile_blocks, BLK, padded), F32),
            pltpu.VMEM((BLK, 128), F32),
            pltpu.VMEM((ny, BLK, 128), F32),
            pltpu.VMEM((BLK, 128), F32),
            pltpu.VMEM((BLK, 128), F32),
            pltpu.VMEM((8, rows // 2), F32),
            pltpu.VMEM((ny, 8, rows // 2), F32),
            pltpu.VMEM((8, rows // 2), F32),
            pltpu.VMEM((8, rows // 2), F32),
            pltpu.VMEM((2, 2, half, 2, share + 8, rows // 2), jnp.int16),
            pltpu.VMEM((2, 2, half, 2, share + 8, rows // 2), jnp.int16),
            pltpu.VMEM((2, share + 8, rows // 2), jnp.int16),
            pltpu.VMEM((2, share + 8, rows // 2), jnp.int16),
            dma((8,)),
            dma((3,)),
            dma, dma, dma((2,)), dma((2,)),
            dma((2,)), dma((2,)), dma((2,)), dma((2,)),
            dma((2, 2, half, 2)), dma((2, 2, half, 2)),
            dma((2,)), dma((2,)),
        ],
        compiler_params=pltpu.CompilerParams(
            collective_id=0, has_side_effects=True, vmem_limit_bytes=60 * 2**20
        ),
        name="tiles",
    )(
        tile_start,
        tile_owner,
        vit_hidden,
        vit_gain,
        vit_bias,
        proj_weight,
        text_emb,
        llm_gain,
        cotangent,
    )
    return (normed, grad_text, grad_vit[:, :share])


def solution(mesh):
    in_specs = (
        P("seq", None),
        P(),
        P(),
        P(None, "mp"),
        P("seq", "mp"),
        P("mp"),
        P("seq", "mp"),
        P(),
        P(),
    )
    out_specs = (P("seq", "mp"), P("seq", "mp"), P("seq", "mp"))
    return jax.shard_map(body, mesh=mesh, in_specs=in_specs, out_specs=out_specs, check_vma=False)
```
